512 devices in a mesh: ra: 16 (over z_lo, core), rb: 32 (over x, y, z_hi).
Axes of the slice: x: 4, y: 4, z: 16 (z_hi: 2, z_lo: 8; z = z_hi * 8 + z_lo), core: 2. Of those that a mesh axis runs over, the one named last changes fastest.
Arguments:
- amplitude: bfloat16 [2, 512, 512, 256], P(None, 'ra', 'rb'), may hold values from -6 to 6
- coupling: bfloat16 [6, 256, 256], replicated, may hold values from -0.5 to 0.5
- pattern: int32 [6, 4, 4], replicated, may hold values 0 or 1
- radial: float32 [6, 512, 512], P(None, 'ra', 'rb'), may hold values from -2.4 to 2.4
- first_prop: bfloat16 [2, 512, 512], replicated, may hold values from -0.1875 to 0.1875
- second_prop: bfloat16 [2, 512, 512], replicated, may hold values from -0.1875 to 0.1875
Outputs:
- evolved: bfloat16 [2, 512, 512, 256], P(None, 'ra', 'rb')
The draws below stay inside these ranges and needn't reach their ends.
All inputs are finite; a program needn't handle non-finite values.
Results may differ from the reference program's by a relative error of at most 0.0095.
Values may be sent and summed in bfloat16 or wider, within the bound.
No kernel may reach another device: no remote copies, remote signals or barrier semaphores. Data moves between devices by JAX's collectives and lax.ppermute only.
A program may use at most 64 MiB of HBM per device.

```python
import jax
import jax.numpy as jnp
from jax import lax

C = 256
BS = 64
NB = 4
KTERMS = 6
N1 = 512
N2 = 512
STEPS = 2


def place_ends(result, key, least, high):
    spot = [jax.random.randint(jax.random.fold_in(key, axis), (), 0, length) for axis, length in enumerate(result.shape)]
    main_axis = result.shape.index(max(result.shape))
    beside = spot[:main_axis] + [(spot[main_axis] + 1) % result.shape[main_axis]] + spot[main_axis + 1:]
    return result.at[tuple(spot)].set(least).at[tuple(beside)].set(high)


def levels(key, shape, cuts, low, largest):
    factor_of = 1.0
    for dim, parts in cuts:
        heights = jax.random.uniform(jax.random.fold_in(jax.random.fold_in(key, 6), dim), (parts,), jnp.float32, low / len(cuts), largest / len(cuts))
        factor_of = factor_of * jnp.repeat(jnp.exp(heights), shape[dim] // parts).reshape((-1,) + (1,) * (len(shape) - 1 - dim))
    return factor_of


def centred(own_key, shape, scale, bound, shards=(), held_as=jnp.bfloat16):
    factor_of = levels(own_key, shape, shards, -0.22, 0.18) if shards else 1.0
    result = jax.random.normal(own_key, shape, jnp.float32) * scale * factor_of
    return jnp.minimum(jnp.maximum(result, -bound), bound).astype(held_as)


def setup_inputs(seed: int = 0) -> dict:
    splits = jax.random.split(jax.random.key(seed), 7)
    amplitude = centred(splits[0], (2, N1, N2, C), 1.0, 6.0, ((1, 16), (2, 32)))
    coupling = centred(splits[1], (KTERMS, C, C), (C // 2) ** -0.5, 0.5)
    pattern = place_ends((jax.random.randint(splits[2], (KTERMS, NB, NB), 0, 2) < 1).astype(jnp.int32), jax.random.fold_in(splits[2], 1), 0, 1)
    radial = centred(splits[3], (KTERMS, N1, N2), 0.4, 2.4, ((1, 16), (2, 32)), jnp.float32)
    first_prop = centred(splits[4], (2, N1, N1), (2 * N1) ** -0.5, 0.1875)
    second_prop = centred(splits[5], (2, N2, N2), (2 * N2) ** -0.5, 0.1875)
    return dict(amplitude=amplitude, coupling=coupling, pattern=pattern, radial=radial, first_prop=first_prop, second_prop=second_prop)


def spread_mask(pattern):
    blocks = pattern.astype(jnp.float32)
    terms, count = blocks.shape[0], blocks.shape[1]
    spread = jnp.broadcast_to(blocks[:, :, None, :, None], (terms, count, BS, count, BS))
    return spread.reshape(terms, count * BS, count * BS)


def couple(amplitude, coupling, block_mask, radial):
    wide = amplitude.astype(jnp.float32)

    def add_term(multipole, summed):
        weights = coupling[multipole].astype(jnp.float32) * block_mask[multipole]
        applied = jnp.einsum("ij,xabj->xabi", weights, wide)
        return summed + applied * radial[multipole][None, :, :, None]

    coupled = lax.fori_loop(0, KTERMS, add_term, jnp.zeros(amplitude.shape, jnp.float32))
    return jnp.stack([wide[0] + coupled[1], wide[1] - coupled[0]]).astype(jnp.bfloat16)


def along_first(amplitude, propagator):
    wide = amplitude.astype(jnp.float32)
    matrix = propagator.astype(jnp.float32)
    real_part = jnp.einsum("ac,cbi->abi", matrix[0], wide[0]) - jnp.einsum("ac,cbi->abi", matrix[1], wide[1])
    imag_part = jnp.einsum("ac,cbi->abi", matrix[0], wide[1]) + jnp.einsum("ac,cbi->abi", matrix[1], wide[0])
    return jnp.stack([real_part, imag_part]).astype(jnp.bfloat16)


def along_second(amplitude, propagator):
    wide = amplitude.astype(jnp.float32)
    matrix = propagator.astype(jnp.float32)
    real_part = jnp.einsum("bc,aci->abi", matrix[0], wide[0]) - jnp.einsum("bc,aci->abi", matrix[1], wide[1])
    imag_part = jnp.einsum("bc,aci->abi", matrix[0], wide[1]) + jnp.einsum("bc,aci->abi", matrix[1], wide[0])
    return jnp.stack([real_part, imag_part]).astype(jnp.bfloat16)


def reference(amplitude, coupling, pattern, radial, first_prop, second_prop):
    block_mask = spread_mask(pattern)
    for sweep in range(STEPS):
        kicked = couple(amplitude, coupling, block_mask, radial)
        half = along_first(kicked, first_prop)
        amplitude = along_second(half, second_prop)
    return amplitude
```

```python
import functools

import jax
import jax.numpy as jnp
from jax import lax
from jax.experimental import pallas as pl
from jax.experimental.pallas import tpu as pltpu
from jax.sharding import PartitionSpec as P

LANES = 128
BF16 = jnp.bfloat16
F32 = jnp.float32


def dot(left, right):
    return jnp.dot(left, right, preferred_element_type=F32)


def dot_rows(left, right):
    return lax.dot_general(left, right, (((1,), (1,)), ((), ())), preferred_element_type=F32)


def swap_blocks(tiles, width):
    count = len(tiles)
    per_tile = LANES // width
    bits = per_tile.bit_length() - 1
    lane = lax.broadcasted_iota(jnp.int32, tiles[0][0].shape, 1)
    for bit in range(bits):
        step = 1 << bit
        shift = width * step
        keep = (lane & shift) == 0
        fresh = list(tiles)
        for m in range(count):
            if m & step:
                continue
            low, high = tiles[m], tiles[m + step]
            fresh[m] = [jnp.where(keep, a, pltpu.roll(b, shift, 1)) for a, b in zip(low, high)]
            fresh[m + step] = [
                jnp.where(keep, pltpu.roll(a, LANES - shift, 1), b) for a, b in zip(low, high)
            ]
        tiles = fresh
    halves = count // per_tile
    return [
        [tiles[h * per_tile + m % per_tile][m // per_tile] for h in range(halves)]
        for m in range(count)
    ]


def masked_weights(coupling_ref, pattern_ref, term, block):
    channels = coupling_ref.shape[1]
    count = channels // block
    lane = lax.broadcasted_iota(jnp.int32, (block, channels), 1)
    rows = []
    for i in range(count):
        mask = jnp.zeros((block, channels), F32)
        for j in range(count):
            inside = (lane >= j * block) & (lane < (j + 1) * block)
            mask = jnp.where(inside, pattern_ref[term, i * count + j].astype(F32), mask)
        piece = coupling_ref[term, i * block:(i + 1) * block, :].astype(F32) * mask
        rows.append(piece.astype(BF16))
    return jnp.concatenate(rows, axis=0)


def kick_into(real, imag, coupling_ref, pattern_ref, factors, block, store):
    terms = coupling_ref.shape[0]
    weights = [masked_weights(coupling_ref, pattern_ref, k, block) for k in range(terms)]
    rows = real.shape[0]
    step = 128
    for start in range(0, rows, step):
        re = real[start:start + step, :]
        im = imag[start:start + step, :]
        sum_re = jnp.zeros(re.shape, F32)
        sum_im = jnp.zeros(re.shape, F32)
        for k in range(terms):
            factor = factors[start:start + step, k:k + 1]
            sum_re = sum_re + dot_rows(re, weights[k]) * factor
            sum_im = sum_im + dot_rows(im, weights[k]) * factor
        store(start, step, re.astype(F32) + sum_im, im.astype(F32) - sum_re)


def first_kick_kernel(groups, cols, amp_ref, coupling_ref, pattern_ref, radial_ref, out_ref, held):
    cells = amp_ref.shape[0] // 2
    channels = amp_ref.shape[1]
    block = channels // 4
    factors = radial_ref[...].T

    def store(start, step, re, im):
        for h in range(channels // LANES):
            held[h, start:start + step, :] = re[:, h * LANES:(h + 1) * LANES]
            held[h, cells + start:cells + start + step, :] = im[:, h * LANES:(h + 1) * LANES]

    kick_into(amp_ref[:cells, :], amp_ref[cells:, :], coupling_ref, pattern_ref, factors, block, store)
    width = channels // groups
    rows = cells // cols
    for part in range(2):
        for a in range(0, rows, 16):
            tiles = []
            for b in range(cols):
                place = pl.ds(part * cells + a * cols + b, 16, stride=cols)
                tiles.append([held[h, place, :] for h in range(channels // LANES)])
            tiles = swap_blocks(tiles, width)
            for g in range(groups):
                out_ref[g, part * rows + a:part * rows + a + 16, :] = jnp.concatenate(
                    tiles[g], axis=1
                ).astype(BF16)


def complex_dot(p_re, p_im, k_re, k_im):
    return dot(p_re, k_re) - dot(p_im, k_im), dot(p_re, k_im) + dot(p_im, k_re)


def first_forward_kernel(prop_ref, piece_ref, out_ref):
    groups, double, lanes = piece_ref.shape
    rows = double // 2
    k_re = piece_ref[:, :rows, :].reshape(groups * rows, lanes)
    k_im = piece_ref[:, rows:, :].reshape(groups * rows, lanes)
    re, im = complex_dot(prop_ref[0], prop_ref[1], k_re, k_im)
    out_ref[:, :lanes] = re.astype(BF16)
    out_ref[:, lanes:] = im.astype(BF16)


def first_back_kernel(prop_ref, piece_ref, out_ref):
    groups, double, lanes = out_ref.shape
    rows = double // 2
    re, im = complex_dot(prop_ref[0], prop_ref[1], piece_ref[:, :lanes], piece_ref[:, lanes:])
    out_ref[:, :rows, :] = re.astype(BF16).reshape(groups, rows, lanes)
    out_ref[:, rows:, :] = im.astype(BF16).reshape(groups, rows, lanes)


def order_kernel(outer, inner, prop_ref, in_ref, out_ref):
    size = prop_ref.shape[1]
    row = lax.broadcasted_iota(jnp.int32, (size, size), 0)
    col = lax.broadcasted_iota(jnp.int32, (size, size), 1)
    place = (row % outer) * inner + row // outer
    move = jnp.where(col == place, 1.0, 0.0).astype(BF16)
    for part in range(2):
        in_ref[part] = dot_rows(prop_ref[part], move).astype(BF16)
        out_ref[part] = dot(move, prop_ref[part]).astype(BF16)


def second_kernel(groups, cols, piece_ref, in_prop_ref, out_prop_ref, coupling_ref, pattern_ref,
                  radial_ref, out_ref, state, kicked):
    channels = coupling_ref.shape[1]
    block = channels // 4
    width = channels // groups
    peers = piece_ref.shape[0] // groups
    lanes = cols * width
    size = peers * cols
    for part in range(2):
        for s in range(0, peers, 16):
            tiles = []
            for g in range(groups):
                piece = piece_ref[g * peers + s:g * peers + s + 16, part * lanes:(part + 1) * lanes]
                piece = piece.astype(F32)
                tiles.append([piece[:, h * LANES:(h + 1) * LANES] for h in range(lanes // LANES)])
            tiles = swap_blocks(tiles, width)
            for b in range(cols):
                state[part, b * peers + s:b * peers + s + 16, :] = jnp.concatenate(
                    tiles[b], axis=1
                ).astype(BF16)
    re, im = complex_dot(in_prop_ref[0], in_prop_ref[1], state[0], state[1])
    factors = radial_ref[...].T

    def store(start, step, new_re, new_im):
        kicked[0, start:start + step, :] = new_re.astype(BF16)
        kicked[1, start:start + step, :] = new_im.astype(BF16)

    kick_into(re.astype(BF16), im.astype(BF16), coupling_ref, pattern_ref, factors, block, store)
    re, im = complex_dot(out_prop_ref[0], out_prop_ref[1], kicked[0], kicked[1])
    state[0] = re.astype(BF16)
    state[1] = im.astype(BF16)
    for part in range(2):
        for s in range(0, peers, 16):
            tiles = []
            for b in range(cols):
                piece = state[part, b * peers + s:b * peers + s + 16, :].astype(F32)
                tiles.append([piece[:, h * LANES:(h + 1) * LANES] for h in range(channels // LANES)])
            tiles = swap_blocks(tiles, width)
            for g in range(groups):
                out_ref[g * peers + s:g * peers + s + 16, part * lanes:(part + 1) * lanes] = (
                    jnp.concatenate(tiles[g], axis=1).astype(BF16)
                )


def last_kernel(groups, cols, piece_ref, out_ref, held):
    channels = out_ref.shape[1]
    cells = out_ref.shape[0] // 2
    rows = cells // cols
    width = channels // groups
    lanes = piece_ref.shape[2]
    for part in range(2):
        for a in range(0, rows, 16):
            tiles = []
            for g in range(groups):
                piece = piece_ref[g, part * rows + a:part * rows + a + 16, :].astype(F32)
                tiles.append([piece[:, h * LANES:(h + 1) * LANES] for h in range(lanes // LANES)])
            tiles = swap_blocks(tiles, width)
            for b in range(cols):
                place = pl.ds(part * cells + a * cols + b, 16, stride=cols)
                for h in range(channels // LANES):
                    held[h, place, :] = tiles[b][h]
    for h in range(channels // LANES):
        out_ref[:, h * LANES:(h + 1) * LANES] = held[h].astype(BF16)


def on_device(amplitude, coupling, pattern, radial, first_prop, second_prop):
    _, rows, cols, channels = amplitude.shape
    cells = rows * cols
    terms, count = pattern.shape[0], pattern.shape[1]
    groups, peers = lax.axis_size("ra"), lax.axis_size("rb")
    width = channels // groups
    lanes = cols * width
    r1, r2 = first_prop.shape[1], second_prop.shape[1]
    params = pltpu.CompilerParams(vmem_limit_bytes=48 * 1024 * 1024)
    vmem = pl.BlockSpec(memory_space=pltpu.VMEM)
    smem = pl.BlockSpec(memory_space=pltpu.SMEM)
    call = functools.partial(pl.pallas_call, compiler_params=params, out_specs=vmem)
    shape = jax.ShapeDtypeStruct
    flat_pattern = pattern.reshape(terms, count * count)

    pad = (-terms) % 8
    here = jnp.pad(radial.reshape(terms, cells), ((0, pad), (0, 0)))
    there = lax.all_to_all(radial, "rb", split_axis=1, concat_axis=2, tiled=True)
    there = jnp.pad(there.reshape(terms, r2), ((0, pad), (0, 0)))

    piece = call(
        functools.partial(first_kick_kernel, groups, cols),
        out_shape=shape((groups, 2 * rows, lanes), BF16),
        in_specs=[vmem, vmem, smem, vmem],
        scratch_shapes=[pltpu.VMEM((channels // LANES, 2 * cells, LANES), F32)],
    )(amplitude.reshape(2 * cells, channels), coupling, flat_pattern, here)
    ordered = pl.pallas_call(
        functools.partial(order_kernel, peers, cols),
        out_shape=[shape((2, r2, r2), BF16)] * 2,
        in_specs=[vmem],
        out_specs=[vmem, vmem],
        compiler_params=params,
    )(second_prop)
    piece = lax.all_to_all(piece, "ra", split_axis=0, concat_axis=0, tiled=True)
    half = call(
        first_forward_kernel,
        out_shape=shape((r1, 2 * lanes), BF16),
        in_specs=[vmem, vmem],
    )(first_prop, piece)
    half = lax.all_to_all(half, ("ra", "rb"), split_axis=0, concat_axis=0, tiled=True)
    half = call(
        functools.partial(second_kernel, groups, cols),
        out_shape=shape((groups * peers, 2 * lanes), BF16),
        in_specs=[vmem, vmem, vmem, vmem, smem, vmem],
        scratch_shapes=[pltpu.VMEM((2, r2, channels), BF16)] * 2,
    )(half, *ordered, coupling, flat_pattern, there)
    half = lax.all_to_all(half, ("ra", "rb"), split_axis=0, concat_axis=0, tiled=True)
    piece = call(
        first_back_kernel,
        out_shape=shape((groups, 2 * rows, lanes), BF16),
        in_specs=[vmem, vmem],
    )(first_prop, half)
    piece = lax.all_to_all(piece, "ra", split_axis=0, concat_axis=0, tiled=True)
    out = call(
        functools.partial(last_kernel, groups, cols),
        out_shape=shape((2 * cells, channels), BF16),
        in_specs=[vmem],
        scratch_shapes=[pltpu.VMEM((channels // LANES, 2 * cells, LANES), F32)],
    )(piece)
    return out.reshape(2, rows, cols, channels)


def solution(mesh):
    return jax.shard_map(
        on_device,
        mesh=mesh,
        in_specs=(P(None, "ra", "rb", None), P(), P(), P(None, "ra", "rb"), P(), P()),
        out_specs=P(None, "ra", "rb", None),
        check_vma=False,
    )
```

```python
import functools

import jax
import jax.numpy as jnp
from jax import lax
from jax.experimental import pallas as pl
from jax.experimental.pallas import tpu as pltpu
from jax.sharding import PartitionSpec as P

LANES = 128
BF16 = jnp.bfloat16
F32 = jnp.float32


def dot(left, right):
    return jnp.dot(left, right, preferred_element_type=F32)


def dot_rows(left, right):
    return lax.dot_general(left, right, (((1,), (1,)), ((), ())), preferred_element_type=F32)


def swap_blocks(tiles, width):
    count = len(tiles)
    per_tile = LANES // width
    bits = per_tile.bit_length() - 1
    lane = lax.broadcasted_iota(jnp.int32, tiles[0][0].shape, 1)
    for bit in range(bits):
        step = 1 << bit
        shift = width * step
        keep = (lane & shift) == 0
        fresh = list(tiles)
        for m in range(count):
            if m & step:
                continue
            low, high = tiles[m], tiles[m + step]
            fresh[m] = [jnp.where(keep, a, pltpu.roll(b, shift, 1)) for a, b in zip(low, high)]
            fresh[m + step] = [
                jnp.where(keep, pltpu.roll(a, LANES - shift, 1), b) for a, b in zip(low, high)
            ]
        tiles = fresh
    halves = count // per_tile
    return [
        [tiles[h * per_tile + m % per_tile][m // per_tile] for h in range(halves)]
        for m in range(count)
    ]


def masked_weights(coupling_ref, pattern_ref, term, block):
    channels = coupling_ref.shape[1]
    count = channels // block
    lane = lax.broadcasted_iota(jnp.int32, (block, channels), 1)
    rows = []
    for i in range(count):
        mask = jnp.zeros((block, channels), F32)
        for j in range(count):
            inside = (lane >= j * block) & (lane < (j + 1) * block)
            mask = jnp.where(inside, pattern_ref[term, i * count + j].astype(F32), mask)
        piece = coupling_ref[term, i * block:(i + 1) * block, :].astype(F32) * mask
        rows.append(piece.astype(BF16))
    return jnp.concatenate(rows, axis=0)


def kick_into(real, imag, coupling_ref, pattern_ref, factors, block, store):
    terms = coupling_ref.shape[0]
    weights = [masked_weights(coupling_ref, pattern_ref, k, block) for k in range(terms)]
    rows = real.shape[0]
    step = 128
    for start in range(0, rows, step):
        re = real[start:start + step, :]
        im = imag[start:start + step, :]
        sum_re = jnp.zeros(re.shape, F32)
        sum_im = jnp.zeros(re.shape, F32)
        for k in range(terms):
            factor = factors[start:start + step, k:k + 1]
            sum_re = sum_re + dot_rows(re, weights[k]) * factor
            sum_im = sum_im + dot_rows(im, weights[k]) * factor
        store(start, step, re.astype(F32) + sum_im, im.astype(F32) - sum_re)


def first_kick_kernel(groups, cols, amp_ref, coupling_ref, pattern_ref, radial_ref, out_ref, held):
    cells = amp_ref.shape[0] // 2
    channels = amp_ref.shape[1]
    block = channels // 4
    factors = radial_ref[...].T

    def store(start, step, re, im):
        for h in range(channels // LANES):
            held[h, start:start + step, :] = re[:, h * LANES:(h + 1) * LANES]
            held[h, cells + start:cells + start + step, :] = im[:, h * LANES:(h + 1) * LANES]

    kick_into(amp_ref[:cells, :], amp_ref[cells:, :], coupling_ref, pattern_ref, factors, block, store)
    width = channels // groups
    rows = cells // cols
    for part in range(2):
        for a in range(0, rows, 16):
            tiles = []
            for b in range(cols):
                place = pl.ds(part * cells + a * cols + b, 16, stride=cols)
                tiles.append([held[h, place, :] for h in range(channels // LANES)])
            tiles = swap_blocks(tiles, width)
            for g in range(groups):
                out_ref[g, part * rows + a:part * rows + a + 16, :] = jnp.concatenate(
                    tiles[g], axis=1
                ).astype(BF16)


def complex_dot(p_re, p_im, k_re, k_im):
    return dot(p_re, k_re) - dot(p_im, k_im), dot(p_re, k_im) + dot(p_im, k_re)


def first_forward_kernel(prop_ref, piece_ref, out_ref):
    groups, double, lanes = piece_ref.shape
    rows = double // 2
    k_re = piece_ref[:, :rows, :].reshape(groups * rows, lanes)
    k_im = piece_ref[:, rows:, :].reshape(groups * rows, lanes)
    re, im = complex_dot(prop_ref[0], prop_ref[1], k_re, k_im)
    out_ref[:, :lanes] = re.astype(BF16)
    out_ref[:, lanes:] = im.astype(BF16)


def first_back_kernel(prop_ref, piece_ref, out_ref):
    groups, double, lanes = out_ref.shape
    rows = double // 2
    re, im = complex_dot(prop_ref[0], prop_ref[1], piece_ref[:, :lanes], piece_ref[:, lanes:])
    out_ref[:, :rows, :] = re.astype(BF16).reshape(groups, rows, lanes)
    out_ref[:, rows:, :] = im.astype(BF16).reshape(groups, rows, lanes)


def order_kernel(outer, inner, prop_ref, in_ref, out_ref):
    size = prop_ref.shape[1]
    row = lax.broadcasted_iota(jnp.int32, (size, size), 0)
    col = lax.broadcasted_iota(jnp.int32, (size, size), 1)
    place = (row % outer) * inner + row // outer
    move = jnp.where(col == place, 1.0, 0.0).astype(BF16)
    for part in range(2):
        in_ref[part] = dot_rows(prop_ref[part], move).astype(BF16)
        out_ref[part] = dot(move, prop_ref[part]).astype(BF16)


def second_kernel(groups, cols, piece_ref, in_prop_ref, out_prop_ref, coupling_ref, pattern_ref,
                  radial_ref, out_ref, state, kicked):
    channels = coupling_ref.shape[1]
    block = channels // 4
    width = channels // groups
    peers = piece_ref.shape[0] // groups
    lanes = cols * width
    size = peers * cols
    for part in range(2):
        for s in range(0, peers, 16):
            tiles = []
            for g in range(groups):
                piece = piece_ref[g * peers + s:g * peers + s + 16, part * lanes:(part + 1) * lanes]
                piece = piece.astype(F32)
                tiles.append([piece[:, h * LANES:(h + 1) * LANES] for h in range(lanes // LANES)])
            tiles = swap_blocks(tiles, width)
            for b in range(cols):
                state[part, b * peers + s:b * peers + s + 16, :] = jnp.concatenate(
                    tiles[b], axis=1
                ).astype(BF16)
    re, im = complex_dot(in_prop_ref[0], in_prop_ref[1], state[0], state[1])
    factors = radial_ref[...].T

    def store(start, step, new_re, new_im):
        kicked[0, start:start + step, :] = new_re.astype(BF16)
        kicked[1, start:start + step, :] = new_im.astype(BF16)

    kick_into(re.astype(BF16), im.astype(BF16), coupling_ref, pattern_ref, factors, block, store)
    re, im = complex_dot(out_prop_ref[0], out_prop_ref[1], kicked[0], kicked[1])
    state[0] = re.astype(BF16)
    state[1] = im.astype(BF16)
    for part in range(2):
        for s in range(0, peers, 16):
            tiles = []
            for b in range(cols):
                piece = state[part, b * peers + s:b * peers + s + 16, :].astype(F32)
                tiles.append([piece[:, h * LANES:(h + 1) * LANES] for h in range(channels // LANES)])
            tiles = swap_blocks(tiles, width)
            for g in range(groups):
                out_ref[g * peers + s:g * peers + s + 16, part * lanes:(part + 1) * lanes] = (
                    jnp.concatenate(tiles[g], axis=1).astype(BF16)
                )


def last_kernel(groups, cols, piece_ref, out_ref, held):
    channels = out_ref.shape[1]
    cells = out_ref.shape[0] // 2
    rows = cells // cols
    width = channels // groups
    lanes = piece_ref.shape[2]
    for part in range(2):
        for a in range(0, rows, 16):
            tiles = []
            for g in range(groups):
                piece = piece_ref[g, part * rows + a:part * rows + a + 16, :].astype(F32)
                tiles.append([piece[:, h * LANES:(h + 1) * LANES] for h in range(lanes // LANES)])
            tiles = swap_blocks(tiles, width)
            for b in range(cols):
                place = pl.ds(part * cells + a * cols + b, 16, stride=cols)
                for h in range(channels // LANES):
                    held[h, place, :] = tiles[b][h]
    for h in range(channels // LANES):
        out_ref[:, h * LANES:(h + 1) * LANES] = held[h].astype(BF16)


def on_device(amplitude, coupling, pattern, radial, first_prop, second_prop):
    _, rows, cols, channels = amplitude.shape
    cells = rows * cols
    terms, count = pattern.shape[0], pattern.shape[1]
    groups, peers = lax.axis_size("ra"), lax.axis_size("rb")
    width = channels // groups
    lanes = cols * width
    r1, r2 = first_prop.shape[1], second_prop.shape[1]
    params = pltpu.CompilerParams(vmem_limit_bytes=48 * 1024 * 1024)
    vmem = pl.BlockSpec(memory_space=pltpu.VMEM)
    smem = pl.BlockSpec(memory_space=pltpu.SMEM)
    call = functools.partial(pl.pallas_call, compiler_params=params, out_specs=vmem)
    shape = jax.ShapeDtypeStruct
    flat_pattern = pattern.reshape(terms, count * count)

    pad = (-terms) % 8
    here = jnp.pad(radial.reshape(terms, cells), ((0, pad), (0, 0)))
    packed = radial.transpose(1, 0, 2).reshape(rows * terms * cols // LANES, LANES)
    everyone = lax.all_gather(jnp.pad(packed, ((0, 64 - packed.shape[0]), (0, 0))), "rb", axis=0, tiled=False)
    mine = everyone[:, :packed.shape[0]].reshape(peers, rows, terms, cols)
    mine = lax.dynamic_index_in_dim(mine, lax.axis_index("rb"), 1, keepdims=False)
    there = jnp.pad(mine.transpose(1, 0, 2).reshape(terms, r2), ((0, pad), (0, 0)))

    piece = call(
        functools.partial(first_kick_kernel, groups, cols),
        out_shape=shape((groups, 2 * rows, lanes), BF16),
        in_specs=[vmem, vmem, smem, vmem],
        scratch_shapes=[pltpu.VMEM((channels // LANES, 2 * cells, LANES), F32)],
    )(amplitude.reshape(2 * cells, channels), coupling, flat_pattern, here)
    ordered = pl.pallas_call(
        functools.partial(order_kernel, peers, cols),
        out_shape=[shape((2, r2, r2), BF16)] * 2,
        in_specs=[vmem],
        out_specs=[vmem, vmem],
        compiler_params=params,
    )(second_prop)
    piece = lax.all_to_all(piece, "ra", split_axis=0, concat_axis=0, tiled=True)
    half = call(
        first_forward_kernel,
        out_shape=shape((r1, 2 * lanes), BF16),
        in_specs=[vmem, vmem],
    )(first_prop, piece)
    half = lax.all_to_all(half, ("ra", "rb"), split_axis=0, concat_axis=0, tiled=True)
    half = call(
        functools.partial(second_kernel, groups, cols),
        out_shape=shape((groups * peers, 2 * lanes), BF16),
        in_specs=[vmem, vmem, vmem, vmem, smem, vmem],
        scratch_shapes=[pltpu.VMEM((2, r2, channels), BF16)] * 2,
    )(half, *ordered, coupling, flat_pattern, there)
    half = lax.all_to_all(half, ("ra", "rb"), split_axis=0, concat_axis=0, tiled=True)
    piece = call(
        first_back_kernel,
        out_shape=shape((groups, 2 * rows, lanes), BF16),
        in_specs=[vmem, vmem],
    )(first_prop, half)
    piece = lax.all_to_all(piece, "ra", split_axis=0, concat_axis=0, tiled=True)
    out = call(
        functools.partial(last_kernel, groups, cols),
        out_shape=shape((2 * cells, channels), BF16),
        in_specs=[vmem],
        scratch_shapes=[pltpu.VMEM((channels // LANES, 2 * cells, LANES), F32)],
    )(piece)
    return out.reshape(2, rows, cols, channels)


def solution(mesh):
    return jax.shard_map(
        on_device,
        mesh=mesh,
        in_specs=(P(None, "ra", "rb", None), P(), P(), P(None, "ra", "rb"), P(), P()),
        out_specs=P(None, "ra", "rb", None),
        check_vma=False,
    )
```

```python
import functools

import jax
import jax.numpy as jnp
from jax import lax
from jax.experimental import pallas as pl
from jax.experimental.pallas import tpu as pltpu
from jax.sharding import PartitionSpec as P

LANES = 128
BF16 = jnp.bfloat16
F32 = jnp.float32


def dot(left, right):
    return jnp.dot(left, right, preferred_element_type=F32)


def dot_rows(left, right):
    return lax.dot_general(left, right, (((1,), (1,)), ((), ())), preferred_element_type=F32)


def swap_blocks(tiles, width):
    count = len(tiles)
    per_tile = LANES // width
    bits = per_tile.bit_length() - 1
    lane = lax.broadcasted_iota(jnp.int32, tiles[0][0].shape, 1)
    for bit in range(bits):
        step = 1 << bit
        shift = width * step
        keep = (lane & shift) == 0
        fresh = list(tiles)
        for m in range(count):
            if m & step:
                continue
            low, high = tiles[m], tiles[m + step]
            fresh[m] = [jnp.where(keep, a, pltpu.roll(b, shift, 1)) for a, b in zip(low, high)]
            fresh[m + step] = [
                jnp.where(keep, pltpu.roll(a, LANES - shift, 1), b) for a, b in zip(low, high)
            ]
        tiles = fresh
    halves = count // per_tile
    return [
        [tiles[h * per_tile + m % per_tile][m // per_tile] for h in range(halves)]
        for m in range(count)
    ]


def masked_weights(coupling_ref, pattern_ref, term, block):
    channels = coupling_ref.shape[1]
    count = channels // block
    lane = lax.broadcasted_iota(jnp.int32, (block, channels), 1)
    rows = []
    for i in range(count):
        mask = jnp.zeros((block, channels), F32)
        for j in range(count):
            inside = (lane >= j * block) & (lane < (j + 1) * block)
            mask = jnp.where(inside, pattern_ref[term, i, j].astype(F32), mask)
        piece = coupling_ref[term, i * block:(i + 1) * block, :].astype(F32) * mask
        rows.append(piece.astype(BF16))
    return jnp.concatenate(rows, axis=0)


def kick_into(load, weights, factor_of, rows, count, store):
    together = max(1, 128 // rows)
    for first in range(0, count, together):
        blocks = range(first, first + together)
        re, im = load(first * rows, together * rows)
        sum_re = jnp.zeros(re.shape, F32)
        sum_im = jnp.zeros(re.shape, F32)
        for k in range(len(weights)):
            factor = jnp.concatenate([factor_of(k, n) for n in blocks], axis=0)
            sum_re = sum_re + dot_rows(re, weights[k]) * factor
            sum_im = sum_im + dot_rows(im, weights[k]) * factor
        store(first * rows, re.astype(F32) + sum_im, im.astype(F32) - sum_re)


def order(prop_ref, out_ref, inner):
    size = prop_ref.shape[1]
    outer = size // inner
    row = lax.broadcasted_iota(jnp.int32, (size, size), 0)
    col = lax.broadcasted_iota(jnp.int32, (size, size), 1)
    place = (row % outer) * inner + row // outer
    move = jnp.where(col == place, 1.0, 0.0).astype(BF16)
    for part in range(2):
        out_ref[part] = dot(move, dot_rows(prop_ref[part], move).astype(BF16)).astype(BF16)


def halves_of(value):
    return [value[:, h * LANES:(h + 1) * LANES] for h in range(value.shape[1] // LANES)]


def first_kick_kernel(groups, amp_ref, coupling_ref, pattern_ref, radial_ref, prop_ref,
                      out_ref, weights_ref, ordered_ref, held, moved, kicked):
    terms, rows, cols = radial_ref.shape
    cells = rows * cols
    channels = coupling_ref.shape[1]
    block = channels // pattern_ref.shape[1]
    parts = channels // LANES
    weights = [masked_weights(coupling_ref, pattern_ref, k, block) for k in range(terms)]
    for k in range(terms):
        weights_ref[k] = weights[k]
    order(prop_ref, ordered_ref, cols)
    for h in range(parts):
        held[h] = amp_ref[:, h * LANES:(h + 1) * LANES].astype(F32)
    for part in range(2):
        for b in range(cols):
            place = pl.ds(part * cells + b, rows, stride=cols)
            moved[part, b * rows:(b + 1) * rows, :] = jnp.concatenate(
                [held[h, place, :] for h in range(parts)], axis=1
            ).astype(BF16)

    def load(start, size):
        return moved[0, start:start + size, :], moved[1, start:start + size, :]

    def store(start, re, im):
        kicked[0, start:start + re.shape[0], :] = re
        kicked[1, start:start + im.shape[0], :] = im

    kick_into(load, weights, lambda k, b: radial_ref[k, :, b:b + 1], rows, cols, store)
    width = channels // groups
    for part in range(2):
        for a in range(0, rows, 16):
            tiles = [
                halves_of(kicked[part, b * rows + a:b * rows + a + 16, :]) for b in range(cols)
            ]
            tiles = swap_blocks(tiles, width)
            for g in range(groups):
                out_ref[g, part * rows + a:part * rows + a + 16, :] = jnp.concatenate(
                    tiles[g], axis=1
                ).astype(BF16)


def complex_dot(p_re, p_im, k_re, k_im):
    return dot(p_re, k_re) - dot(p_im, k_im), dot(p_re, k_im) + dot(p_im, k_re)


def first_forward_kernel(prop_ref, piece_ref, out_ref):
    groups, double, lanes = piece_ref.shape
    rows = double // 2
    k_re = piece_ref[:, :rows, :].reshape(groups * rows, lanes)
    k_im = piece_ref[:, rows:, :].reshape(groups * rows, lanes)
    re, im = complex_dot(prop_ref[0], prop_ref[1], k_re, k_im)
    out_ref[:, :lanes] = re.astype(BF16)
    out_ref[:, lanes:] = im.astype(BF16)


def first_back_kernel(prop_ref, piece_ref, out_ref):
    groups, double, lanes = out_ref.shape
    rows = double // 2
    re, im = complex_dot(prop_ref[0], prop_ref[1], piece_ref[:, :lanes], piece_ref[:, lanes:])
    out_ref[:, :rows, :] = re.astype(BF16).reshape(groups, rows, lanes)
    out_ref[:, rows:, :] = im.astype(BF16).reshape(groups, rows, lanes)


def second_kernel(groups, cols, piece_ref, prop_ref, weights_ref, radial_ref, out_ref, state, kicked):
    terms, channels = weights_ref.shape[0], weights_ref.shape[1]
    width = channels // groups
    peers = piece_ref.shape[0] // groups
    lanes = cols * width
    size = peers * cols
    for part in range(2):
        for s in range(0, peers, 16):
            tiles = []
            for g in range(groups):
                piece = piece_ref[g * peers + s:g * peers + s + 16, part * lanes:(part + 1) * lanes]
                piece = piece.astype(F32)
                tiles.append([piece[:, h * LANES:(h + 1) * LANES] for h in range(lanes // LANES)])
            tiles = swap_blocks(tiles, width)
            for b in range(cols):
                state[part, b * peers + s:b * peers + s + 16, :] = jnp.concatenate(
                    tiles[b], axis=1
                ).astype(BF16)
    re, im = complex_dot(prop_ref[0], prop_ref[1], state[0], state[1])
    state[0] = re.astype(BF16)
    state[1] = im.astype(BF16)

    def load(start, size):
        return state[0, start:start + size, :], state[1, start:start + size, :]

    def store(start, new_re, new_im):
        kicked[0, start:start + new_re.shape[0], :] = new_re.astype(BF16)
        kicked[1, start:start + new_im.shape[0], :] = new_im.astype(BF16)

    weights = [weights_ref[k] for k in range(terms)]
    kick_into(
        load, weights, lambda k, b: radial_ref[:, k * cols + b:k * cols + b + 1], peers, cols, store
    )
    re, im = complex_dot(prop_ref[0], prop_ref[1], kicked[0], kicked[1])
    state[0] = re.astype(BF16)
    state[1] = im.astype(BF16)
    for part in range(2):
        for s in range(0, peers, 16):
            tiles = []
            for b in range(cols):
                piece = state[part, b * peers + s:b * peers + s + 16, :].astype(F32)
                tiles.append([piece[:, h * LANES:(h + 1) * LANES] for h in range(channels // LANES)])
            tiles = swap_blocks(tiles, width)
            for g in range(groups):
                out_ref[g * peers + s:g * peers + s + 16, part * lanes:(part + 1) * lanes] = (
                    jnp.concatenate(tiles[g], axis=1).astype(BF16)
                )


def last_kernel(groups, cols, piece_ref, out_ref, held):
    channels = out_ref.shape[1]
    cells = out_ref.shape[0] // 2
    rows = cells // cols
    width = channels // groups
    lanes = piece_ref.shape[2]
    for part in range(2):
        for a in range(0, rows, 16):
            tiles = []
            for g in range(groups):
                piece = piece_ref[g, part * rows + a:part * rows + a + 16, :].astype(F32)
                tiles.append([piece[:, h * LANES:(h + 1) * LANES] for h in range(lanes // LANES)])
            tiles = swap_blocks(tiles, width)
            for b in range(cols):
                place = pl.ds(part * cells + a * cols + b, 16, stride=cols)
                for h in range(channels // LANES):
                    held[h, place, :] = tiles[b][h]
    for h in range(channels // LANES):
        out_ref[:, h * LANES:(h + 1) * LANES] = held[h].astype(BF16)


def on_device(amplitude, coupling, pattern, radial, first_prop, second_prop):
    _, rows, cols, channels = amplitude.shape
    cells = rows * cols
    terms = pattern.shape[0]
    groups, peers = lax.axis_size("ra"), lax.axis_size("rb")
    width = channels // groups
    lanes = cols * width
    r1, r2 = first_prop.shape[1], second_prop.shape[1]
    params = pltpu.CompilerParams(vmem_limit_bytes=48 * 1024 * 1024)
    vmem = pl.BlockSpec(memory_space=pltpu.VMEM)
    smem = pl.BlockSpec(memory_space=pltpu.SMEM)
    call = functools.partial(pl.pallas_call, compiler_params=params, out_specs=vmem)
    shape = jax.ShapeDtypeStruct

    packed = radial.transpose(1, 0, 2).reshape(rows, terms * cols)
    packed = jnp.pad(packed, ((0, 0), (0, (-terms * cols) % LANES)))
    packed = lax.all_to_all(packed, "rb", split_axis=0, concat_axis=0, tiled=True)

    piece, weights, ordered = pl.pallas_call(
        functools.partial(first_kick_kernel, groups),
        out_shape=[
            shape((groups, 2 * rows, lanes), BF16),
            shape(coupling.shape, BF16),
            shape(second_prop.shape, BF16),
        ],
        in_specs=[vmem, vmem, smem, vmem, vmem],
        out_specs=[vmem] * 3,
        scratch_shapes=[
            pltpu.VMEM((channels // LANES, 2 * cells, LANES), F32),
            pltpu.VMEM((2, cells, channels), BF16),
            pltpu.VMEM((2, cells, channels), F32),
        ],
        compiler_params=params,
    )(amplitude.reshape(2 * cells, channels), coupling, pattern, radial, second_prop)
    piece, packed = lax.optimization_barrier((piece, packed))
    piece = lax.all_to_all(piece, "ra", split_axis=0, concat_axis=0, tiled=True)
    half = call(
        first_forward_kernel,
        out_shape=shape((r1, 2 * lanes), BF16),
        in_specs=[vmem, vmem],
    )(first_prop, piece)
    half = lax.all_to_all(half, ("ra", "rb"), split_axis=0, concat_axis=0, tiled=True)
    half = call(
        functools.partial(second_kernel, groups, cols),
        out_shape=shape((groups * peers, 2 * lanes), BF16),
        in_specs=[vmem] * 4,
        scratch_shapes=[pltpu.VMEM((2, r2, channels), BF16)] * 2,
    )(half, ordered, weights, packed)
    half = lax.all_to_all(half, ("ra", "rb"), split_axis=0, concat_axis=0, tiled=True)
    piece = call(
        first_back_kernel,
        out_shape=shape((groups, 2 * rows, lanes), BF16),
        in_specs=[vmem, vmem],
    )(first_prop, half)
    piece = lax.all_to_all(piece, "ra", split_axis=0, concat_axis=0, tiled=True)
    out = call(
        functools.partial(last_kernel, groups, cols),
        out_shape=shape((2 * cells, channels), BF16),
        in_specs=[vmem],
        scratch_shapes=[pltpu.VMEM((channels // LANES, 2 * cells, LANES), F32)],
    )(piece)
    return out.reshape(2, rows, cols, channels)


def solution(mesh):
    return jax.shard_map(
        on_device,
        mesh=mesh,
        in_specs=(P(None, "ra", "rb", None), P(), P(), P(None, "ra", "rb"), P(), P()),
        out_specs=P(None, "ra", "rb", None),
        check_vma=False,
    )
```

```python
import functools

import jax
import jax.numpy as jnp
from jax import lax
from jax.experimental import pallas as pl
from jax.experimental.pallas import tpu as pltpu
from jax.sharding import PartitionSpec as P

LANES = 128
BF16 = jnp.bfloat16
F32 = jnp.float32


def dot(left, right):
    return jnp.dot(left, right, preferred_element_type=F32)


def dot_rows(left, right):
    return lax.dot_general(left, right, (((1,), (1,)), ((), ())), preferred_element_type=F32)


def swap_blocks(tiles, width):
    count = len(tiles)
    per_tile = LANES // width
    bits = per_tile.bit_length() - 1
    lane = lax.broadcasted_iota(jnp.int32, tiles[0][0].shape, 1)
    for bit in range(bits):
        step = 1 << bit
        shift = width * step
        keep = (lane & shift) == 0
        fresh = list(tiles)
        for m in range(count):
            if m & step:
                continue
            low, high = tiles[m], tiles[m + step]
            fresh[m] = [jnp.where(keep, a, pltpu.roll(b, shift, 1)) for a, b in zip(low, high)]
            fresh[m + step] = [
                jnp.where(keep, pltpu.roll(a, LANES - shift, 1), b) for a, b in zip(low, high)
            ]
        tiles = fresh
    halves = count // per_tile
    return [
        [tiles[h * per_tile + m % per_tile][m // per_tile] for h in range(halves)]
        for m in range(count)
    ]


def masked_weights(coupling_ref, pattern_ref, term, block):
    channels = coupling_ref.shape[1]
    count = channels // block
    lane = lax.broadcasted_iota(jnp.int32, (block, channels), 1)
    rows = []
    for i in range(count):
        mask = jnp.zeros((block, channels), F32)
        for j in range(count):
            inside = (lane >= j * block) & (lane < (j + 1) * block)
            mask = jnp.where(inside, pattern_ref[term, i, j].astype(F32), mask)
        piece = coupling_ref[term, i * block:(i + 1) * block, :].astype(F32) * mask
        rows.append(piece.astype(BF16))
    return jnp.concatenate(rows, axis=0)


def kick_into(load, weights, factor_of, rows, count, store):
    together = max(1, 128 // rows)
    for first in range(0, count, together):
        blocks = range(first, first + together)
        re, im = load(first * rows, together * rows)
        sum_re = jnp.zeros(re.shape, F32)
        sum_im = jnp.zeros(re.shape, F32)
        for k in range(len(weights)):
            factor = jnp.concatenate([factor_of(k, n) for n in blocks], axis=0)
            sum_re = sum_re + dot_rows(re, weights[k]) * factor
            sum_im = sum_im + dot_rows(im, weights[k]) * factor
        store(first * rows, re.astype(F32) + sum_im, im.astype(F32) - sum_re)


def order(prop_ref, out_ref, inner):
    size = prop_ref.shape[1]
    outer = size // inner
    row = lax.broadcasted_iota(jnp.int32, (size, size), 0)
    col = lax.broadcasted_iota(jnp.int32, (size, size), 1)
    place = (row % outer) * inner + row // outer
    move = jnp.where(col == place, 1.0, 0.0).astype(BF16)
    for part in range(2):
        out_ref[part] = dot(move, dot_rows(prop_ref[part], move).astype(BF16)).astype(BF16)


def halves_of(value):
    return [value[:, h * LANES:(h + 1) * LANES] for h in range(value.shape[1] // LANES)]


def tables_kernel(inner, coupling_ref, pattern_ref, prop_ref, weights_ref, ordered_ref):
    block = coupling_ref.shape[1] // pattern_ref.shape[1]
    for k in range(coupling_ref.shape[0]):
        weights_ref[k] = masked_weights(coupling_ref, pattern_ref, k, block)
    order(prop_ref, ordered_ref, inner)


def first_kick_kernel(groups, amp_ref, weights_ref, radial_ref, out_ref, held, moved, kicked):
    terms, rows, cols = radial_ref.shape
    cells = rows * cols
    channels = weights_ref.shape[1]
    parts = channels // LANES
    weights = [weights_ref[k] for k in range(terms)]
    for h in range(parts):
        held[h] = amp_ref[:, h * LANES:(h + 1) * LANES].astype(F32)
    for part in range(2):
        for b in range(cols):
            place = pl.ds(part * cells + b, rows, stride=cols)
            moved[part, b * rows:(b + 1) * rows, :] = jnp.concatenate(
                [held[h, place, :] for h in range(parts)], axis=1
            ).astype(BF16)

    def load(start, size):
        return moved[0, start:start + size, :], moved[1, start:start + size, :]

    def store(start, re, im):
        kicked[0, start:start + re.shape[0], :] = re
        kicked[1, start:start + im.shape[0], :] = im

    kick_into(load, weights, lambda k, b: radial_ref[k, :, b:b + 1], rows, cols, store)
    width = channels // groups
    for part in range(2):
        for a in range(0, rows, 16):
            tiles = [
                halves_of(kicked[part, b * rows + a:b * rows + a + 16, :]) for b in range(cols)
            ]
            tiles = swap_blocks(tiles, width)
            for g in range(groups):
                out_ref[g, part * rows + a:part * rows + a + 16, :] = jnp.concatenate(
                    tiles[g], axis=1
                ).astype(BF16)


def complex_dot(p_re, p_im, k_re, k_im):
    return dot(p_re, k_re) - dot(p_im, k_im), dot(p_re, k_im) + dot(p_im, k_re)


def first_forward_kernel(prop_ref, piece_ref, out_ref):
    groups, double, lanes = piece_ref.shape
    rows = double // 2
    k_re = piece_ref[:, :rows, :].reshape(groups * rows, lanes)
    k_im = piece_ref[:, rows:, :].reshape(groups * rows, lanes)
    re, im = complex_dot(prop_ref[0], prop_ref[1], k_re, k_im)
    out_ref[:, 0, :] = re.astype(BF16)
    out_ref[:, 1, :] = im.astype(BF16)


def first_back_kernel(prop_ref, piece_ref, out_ref):
    groups, double, lanes = out_ref.shape
    rows = double // 2
    re, im = complex_dot(prop_ref[0], prop_ref[1], piece_ref[:, 0, :], piece_ref[:, 1, :])
    out_ref[:, :rows, :] = re.astype(BF16).reshape(groups, rows, lanes)
    out_ref[:, rows:, :] = im.astype(BF16).reshape(groups, rows, lanes)


def second_kernel(groups, cols, piece_ref, prop_ref, weights_ref, radial_ref, out_ref, state, kicked):
    terms, channels = weights_ref.shape[0], weights_ref.shape[1]
    width = channels // groups
    peers = piece_ref.shape[0] // groups
    lanes = cols * width
    size = peers * cols
    for part in range(2):
        for s in range(0, peers, 16):
            tiles = []
            for g in range(groups):
                piece = piece_ref[g * peers + s:g * peers + s + 16, part, :]
                piece = piece.astype(F32)
                tiles.append([piece[:, h * LANES:(h + 1) * LANES] for h in range(lanes // LANES)])
            tiles = swap_blocks(tiles, width)
            for b in range(cols):
                state[part, b * peers + s:b * peers + s + 16, :] = jnp.concatenate(
                    tiles[b], axis=1
                ).astype(BF16)
    re, im = complex_dot(prop_ref[0], prop_ref[1], state[0], state[1])
    state[0] = re.astype(BF16)
    state[1] = im.astype(BF16)

    def load(start, size):
        return state[0, start:start + size, :], state[1, start:start + size, :]

    def store(start, new_re, new_im):
        kicked[0, start:start + new_re.shape[0], :] = new_re.astype(BF16)
        kicked[1, start:start + new_im.shape[0], :] = new_im.astype(BF16)

    weights = [weights_ref[k] for k in range(terms)]
    kick_into(
        load, weights, lambda k, b: radial_ref[:, k * cols + b:k * cols + b + 1], peers, cols, store
    )
    re, im = complex_dot(prop_ref[0], prop_ref[1], kicked[0], kicked[1])
    state[0] = re.astype(BF16)
    state[1] = im.astype(BF16)
    for part in range(2):
        for s in range(0, peers, 16):
            tiles = []
            for b in range(cols):
                piece = state[part, b * peers + s:b * peers + s + 16, :].astype(F32)
                tiles.append([piece[:, h * LANES:(h + 1) * LANES] for h in range(channels // LANES)])
            tiles = swap_blocks(tiles, width)
            for g in range(groups):
                out_ref[g * peers + s:g * peers + s + 16, part, :] = (
                    jnp.concatenate(tiles[g], axis=1).astype(BF16)
                )


def last_kernel(groups, cols, piece_ref, out_ref, held):
    channels = out_ref.shape[1]
    cells = out_ref.shape[0] // 2
    rows = cells // cols
    width = channels // groups
    lanes = piece_ref.shape[2]
    for part in range(2):
        for a in range(0, rows, 16):
            tiles = []
            for g in range(groups):
                piece = piece_ref[g, part * rows + a:part * rows + a + 16, :].astype(F32)
                tiles.append([piece[:, h * LANES:(h + 1) * LANES] for h in range(lanes // LANES)])
            tiles = swap_blocks(tiles, width)
            for b in range(cols):
                place = pl.ds(part * cells + a * cols + b, 16, stride=cols)
                for h in range(channels // LANES):
                    held[h, place, :] = tiles[b][h]
    for h in range(channels // LANES):
        out_ref[:, h * LANES:(h + 1) * LANES] = held[h].astype(BF16)


def swap_rows(table, axis, step, last):
    size = table.shape[0]
    me = lax.axis_index(axis)
    while step >= last:
        pairs = [(i, i ^ step) for i in range(size)]
        split = table.reshape(size // (2 * step), 2, step, table.shape[1])
        low, high = split[:, 0], split[:, 1]
        upper = (me & step) != 0
        other = lax.ppermute(jnp.where(upper, low, high), axis, pairs)
        low, high = jnp.where(upper, other, low), jnp.where(upper, high, other)
        table = jnp.stack([low, high], axis=1).reshape(table.shape)
        step //= 2
    return table


def on_device(amplitude, coupling, pattern, radial, first_prop, second_prop):
    _, rows, cols, channels = amplitude.shape
    cells = rows * cols
    terms = pattern.shape[0]
    groups, peers = lax.axis_size("ra"), lax.axis_size("rb")
    width = channels // groups
    lanes = cols * width
    r1, r2 = first_prop.shape[1], second_prop.shape[1]
    params = pltpu.CompilerParams(vmem_limit_bytes=20 * 1024 * 1024)
    vmem = pl.BlockSpec(memory_space=pltpu.VMEM)
    smem = pl.BlockSpec(memory_space=pltpu.SMEM)
    call = functools.partial(pl.pallas_call, compiler_params=params, out_specs=vmem)
    shape = jax.ShapeDtypeStruct

    packed = radial.transpose(1, 0, 2).reshape(rows, terms * cols)
    packed = jnp.pad(packed, ((0, 0), (0, (-terms * cols) % LANES)))

    weights, ordered = pl.pallas_call(
        functools.partial(tables_kernel, cols),
        out_shape=[shape(coupling.shape, BF16), shape(second_prop.shape, BF16)],
        in_specs=[vmem, smem, vmem],
        out_specs=[vmem] * 2,
        compiler_params=params,
    )(coupling, pattern, second_prop)
    packed = swap_rows(packed, "rb", peers // 2, peers // 2)
    packed, weights = lax.optimization_barrier((packed, weights))
    packed = swap_rows(packed, "rb", peers // 4, 1)
    piece = call(
        functools.partial(first_kick_kernel, groups),
        out_shape=shape((groups, 2 * rows, lanes), BF16),
        in_specs=[vmem] * 3,
        scratch_shapes=[
            pltpu.VMEM((channels // LANES, 2 * cells, LANES), F32),
            pltpu.VMEM((2, cells, channels), BF16),
            pltpu.VMEM((2, cells, channels), F32),
        ],
    )(amplitude.reshape(2 * cells, channels), weights, radial)
    piece = lax.all_to_all(piece, "ra", split_axis=0, concat_axis=0, tiled=True)
    half = call(
        first_forward_kernel,
        out_shape=shape((r1, 2, lanes), BF16),
        in_specs=[vmem, vmem],
    )(first_prop, piece)
    half, packed = lax.optimization_barrier((half, packed))
    half = lax.all_to_all(half, ("ra", "rb"), split_axis=0, concat_axis=0, tiled=True)
    half = call(
        functools.partial(second_kernel, groups, cols),
        out_shape=shape((groups * peers, 2, lanes), BF16),
        in_specs=[vmem] * 4,
        scratch_shapes=[pltpu.VMEM((2, r2, channels), BF16)] * 2,
    )(half, ordered, weights, packed)
    half = lax.all_to_all(half, ("ra", "rb"), split_axis=0, concat_axis=0, tiled=True)
    piece = call(
        first_back_kernel,
        out_shape=shape((groups, 2 * rows, lanes), BF16),
        in_specs=[vmem, vmem],
    )(first_prop, half)
    piece = lax.all_to_all(piece, "ra", split_axis=0, concat_axis=0, tiled=True)
    out = call(
        functools.partial(last_kernel, groups, cols),
        out_shape=shape((2 * cells, channels), BF16),
        in_specs=[vmem],
        scratch_shapes=[pltpu.VMEM((channels // LANES, 2 * cells, LANES), F32)],
    )(piece)
    return out.reshape(2, rows, cols, channels)


def solution(mesh):
    return jax.shard_map(
        on_device,
        mesh=mesh,
        in_specs=(P(None, "ra", "rb", None), P(), P(), P(None, "ra", "rb"), P(), P()),
        out_specs=P(None, "ra", "rb", None),
        check_vma=False,
    )
```

```python
import functools

import jax
import jax.numpy as jnp
from jax import lax
from jax.experimental import pallas as pl
from jax.experimental.pallas import tpu as pltpu
from jax.sharding import PartitionSpec as P

LANES = 128
BF16 = jnp.bfloat16
F32 = jnp.float32


def dot(left, right):
    return jnp.dot(left, right, preferred_element_type=F32)


def dot_rows(left, right):
    return lax.dot_general(left, right, (((1,), (1,)), ((), ())), preferred_element_type=F32)


def swap_blocks(tiles, width):
    count = len(tiles)
    per_tile = LANES // width
    bits = per_tile.bit_length() - 1
    lane = lax.broadcasted_iota(jnp.int32, tiles[0][0].shape, 1)
    for bit in range(bits):
        step = 1 << bit
        shift = width * step
        keep = (lane & shift) == 0
        fresh = list(tiles)
        for m in range(count):
            if m & step:
                continue
            low, high = tiles[m], tiles[m + step]
            fresh[m] = [jnp.where(keep, a, pltpu.roll(b, shift, 1)) for a, b in zip(low, high)]
            fresh[m + step] = [
                jnp.where(keep, pltpu.roll(a, LANES - shift, 1), b) for a, b in zip(low, high)
            ]
        tiles = fresh
    halves = count // per_tile
    return [
        [tiles[h * per_tile + m % per_tile][m // per_tile] for h in range(halves)]
        for m in range(count)
    ]


def masked_weights(coupling_ref, pattern_ref, term, block):
    channels = coupling_ref.shape[1]
    count = channels // block
    lane = lax.broadcasted_iota(jnp.int32, (block, channels), 1)
    rows = []
    for i in range(count):
        mask = jnp.zeros((block, channels), F32)
        for j in range(count):
            inside = (lane >= j * block) & (lane < (j + 1) * block)
            mask = jnp.where(inside, pattern_ref[term, i, j].astype(F32), mask)
        piece = coupling_ref[term, i * block:(i + 1) * block, :].astype(F32) * mask
        rows.append(piece.astype(BF16))
    return jnp.concatenate(rows, axis=0)


def kick_into(load, weights, factor_of, rows, count, store):
    together = max(1, 128 // rows)
    for first in range(0, count, together):
        blocks = range(first, first + together)
        re, im = load(first * rows, together * rows)
        sum_re = jnp.zeros(re.shape, F32)
        sum_im = jnp.zeros(re.shape, F32)
        for k in range(len(weights)):
            factor = jnp.concatenate([factor_of(k, n) for n in blocks], axis=0)
            sum_re = sum_re + dot_rows(re, weights[k]) * factor
            sum_im = sum_im + dot_rows(im, weights[k]) * factor
        store(first * rows, re.astype(F32) + sum_im, im.astype(F32) - sum_re)


def order(prop_ref, out_ref, inner):
    size = prop_ref.shape[1]
    outer = size // inner
    row = lax.broadcasted_iota(jnp.int32, (size, size), 0)
    col = lax.broadcasted_iota(jnp.int32, (size, size), 1)
    place = (row % outer) * inner + row // outer
    move = jnp.where(col == place, 1.0, 0.0).astype(BF16)
    for part in range(2):
        out_ref[part] = dot(move, dot_rows(prop_ref[part], move).astype(BF16)).astype(BF16)


def halves_of(value):
    return [value[:, h * LANES:(h + 1) * LANES] for h in range(value.shape[1] // LANES)]


def order_kernel(inner, prop_ref, ordered_ref):
    order(prop_ref, ordered_ref, inner)


def first_kick_kernel(groups, amp_ref, coupling_ref, pattern_ref, radial_ref, out_ref, weights_ref,
                      held, moved, kicked):
    terms, rows, cols = radial_ref.shape
    cells = rows * cols
    channels = coupling_ref.shape[1]
    block = channels // pattern_ref.shape[1]
    parts = channels // LANES
    weights = [masked_weights(coupling_ref, pattern_ref, k, block) for k in range(terms)]
    for k in range(terms):
        weights_ref[k] = weights[k]
    for h in range(parts):
        held[h] = amp_ref[:, h * LANES:(h + 1) * LANES].astype(F32)
    for part in range(2):
        for b in range(cols):
            place = pl.ds(part * cells + b, rows, stride=cols)
            moved[part, b * rows:(b + 1) * rows, :] = jnp.concatenate(
                [held[h, place, :] for h in range(parts)], axis=1
            ).astype(BF16)

    def load(start, size):
        return moved[0, start:start + size, :], moved[1, start:start + size, :]

    def store(start, re, im):
        kicked[0, start:start + re.shape[0], :] = re
        kicked[1, start:start + im.shape[0], :] = im

    kick_into(load, weights, lambda k, b: radial_ref[k, :, b:b + 1], rows, cols, store)
    width = channels // groups
    for part in range(2):
        for a in range(0, rows, 16):
            tiles = [
                halves_of(kicked[part, b * rows + a:b * rows + a + 16, :]) for b in range(cols)
            ]
            tiles = swap_blocks(tiles, width)
            for g in range(groups):
                out_ref[g, part * rows + a:part * rows + a + 16, :] = jnp.concatenate(
                    tiles[g], axis=1
                ).astype(BF16)


def complex_dot(p_re, p_im, k_re, k_im):
    return dot(p_re, k_re) - dot(p_im, k_im), dot(p_re, k_im) + dot(p_im, k_re)


def first_forward_kernel(prop_ref, piece_ref, out_ref):
    groups, double, lanes = piece_ref.shape
    rows = double // 2
    k_re = piece_ref[:, :rows, :].reshape(groups * rows, lanes)
    k_im = piece_ref[:, rows:, :].reshape(groups * rows, lanes)
    re, im = complex_dot(prop_ref[0], prop_ref[1], k_re, k_im)
    out_ref[:, 0, :] = re.astype(BF16)
    out_ref[:, 1, :] = im.astype(BF16)


def first_back_kernel(prop_ref, piece_ref, out_ref):
    groups, double, lanes = out_ref.shape
    rows = double // 2
    re, im = complex_dot(prop_ref[0], prop_ref[1], piece_ref[:, 0, :], piece_ref[:, 1, :])
    out_ref[:, :rows, :] = re.astype(BF16).reshape(groups, rows, lanes)
    out_ref[:, rows:, :] = im.astype(BF16).reshape(groups, rows, lanes)


def second_kernel(groups, cols, piece_ref, prop_ref, weights_ref, radial_ref, out_ref, state, kicked):
    terms, channels = weights_ref.shape[0], weights_ref.shape[1]
    width = channels // groups
    peers = piece_ref.shape[0] // groups
    lanes = cols * width
    size = peers * cols
    for part in range(2):
        for s in range(0, peers, 16):
            tiles = []
            for g in range(groups):
                piece = piece_ref[g * peers + s:g * peers + s + 16, part, :]
                piece = piece.astype(F32)
                tiles.append([piece[:, h * LANES:(h + 1) * LANES] for h in range(lanes // LANES)])
            tiles = swap_blocks(tiles, width)
            for b in range(cols):
                state[part, b * peers + s:b * peers + s + 16, :] = jnp.concatenate(
                    tiles[b], axis=1
                ).astype(BF16)
    re, im = complex_dot(prop_ref[0], prop_ref[1], state[0], state[1])
    state[0] = re.astype(BF16)
    state[1] = im.astype(BF16)

    def load(start, size):
        return state[0, start:start + size, :], state[1, start:start + size, :]

    def store(start, new_re, new_im):
        kicked[0, start:start + new_re.shape[0], :] = new_re.astype(BF16)
        kicked[1, start:start + new_im.shape[0], :] = new_im.astype(BF16)

    weights = [weights_ref[k] for k in range(terms)]
    kick_into(
        load, weights, lambda k, b: radial_ref[:, k * cols + b:k * cols + b + 1], peers, cols, store
    )
    re, im = complex_dot(prop_ref[0], prop_ref[1], kicked[0], kicked[1])
    state[0] = re.astype(BF16)
    state[1] = im.astype(BF16)
    for part in range(2):
        for s in range(0, peers, 16):
            tiles = []
            for b in range(cols):
                piece = state[part, b * peers + s:b * peers + s + 16, :].astype(F32)
                tiles.append([piece[:, h * LANES:(h + 1) * LANES] for h in range(channels // LANES)])
            tiles = swap_blocks(tiles, width)
            for g in range(groups):
                out_ref[g * peers + s:g * peers + s + 16, part, :] = (
                    jnp.concatenate(tiles[g], axis=1).astype(BF16)
                )


def last_kernel(groups, cols, piece_ref, out_ref, held):
    channels = out_ref.shape[1]
    cells = out_ref.shape[0] // 2
    rows = cells // cols
    width = channels // groups
    lanes = piece_ref.shape[2]
    for part in range(2):
        for a in range(0, rows, 16):
            tiles = []
            for g in range(groups):
                piece = piece_ref[g, part * rows + a:part * rows + a + 16, :].astype(F32)
                tiles.append([piece[:, h * LANES:(h + 1) * LANES] for h in range(lanes // LANES)])
            tiles = swap_blocks(tiles, width)
            for b in range(cols):
                place = pl.ds(part * cells + a * cols + b, 16, stride=cols)
                for h in range(channels // LANES):
                    held[h, place, :] = tiles[b][h]
    for h in range(channels // LANES):
        out_ref[:, h * LANES:(h + 1) * LANES] = held[h].astype(BF16)


def swap_rows(table, axis, steps):
    size = table.shape[0]
    me = lax.axis_index(axis)
    for step in steps:
        pairs = [(i, i ^ step) for i in range(size)]
        split = table.reshape(size // (2 * step), 2, step, table.shape[1])
        low, high = split[:, 0], split[:, 1]
        upper = (me & step) != 0
        other = lax.ppermute(jnp.where(upper, low, high), axis, pairs)
        low, high = jnp.where(upper, other, low), jnp.where(upper, high, other)
        table = jnp.stack([low, high], axis=1).reshape(table.shape)
    return table


def on_device(amplitude, coupling, pattern, radial, first_prop, second_prop):
    _, rows, cols, channels = amplitude.shape
    cells = rows * cols
    terms = pattern.shape[0]
    groups, peers = lax.axis_size("ra"), lax.axis_size("rb")
    width = channels // groups
    lanes = cols * width
    r1, r2 = first_prop.shape[1], second_prop.shape[1]
    params = pltpu.CompilerParams(vmem_limit_bytes=20 * 1024 * 1024)
    vmem = pl.BlockSpec(memory_space=pltpu.VMEM)
    smem = pl.BlockSpec(memory_space=pltpu.SMEM)
    call = functools.partial(pl.pallas_call, compiler_params=params, out_specs=vmem)
    shape = jax.ShapeDtypeStruct

    packed = radial.transpose(1, 0, 2).reshape(rows, terms * cols)
    packed = jnp.pad(packed, ((0, 0), (0, (-terms * cols) % LANES)))

    packed = swap_rows(packed, "rb", [1])
    piece, weights = pl.pallas_call(
        functools.partial(first_kick_kernel, groups),
        out_shape=[shape((groups, 2 * rows, lanes), BF16), shape(coupling.shape, BF16)],
        in_specs=[vmem, vmem, smem, vmem],
        out_specs=[vmem] * 2,
        scratch_shapes=[
            pltpu.VMEM((channels // LANES, 2 * cells, LANES), F32),
            pltpu.VMEM((2, cells, channels), BF16),
            pltpu.VMEM((2, cells, channels), F32),
        ],
        compiler_params=params,
    )(amplitude.reshape(2 * cells, channels), coupling, pattern, radial)
    packed, weights, second_prop = lax.optimization_barrier((packed, weights, second_prop))
    steps = [1 << bit for bit in range(1, peers.bit_length() - 1)]
    packed = swap_rows(packed, "rb", steps[::-1])
    ordered = call(
        functools.partial(order_kernel, cols),
        out_shape=shape(second_prop.shape, BF16),
        in_specs=[vmem],
    )(second_prop)
    piece = lax.all_to_all(piece, "ra", split_axis=0, concat_axis=0, tiled=True)
    half = call(
        first_forward_kernel,
        out_shape=shape((r1, 2, lanes), BF16),
        in_specs=[vmem, vmem],
    )(first_prop, piece)
    half, packed, ordered = lax.optimization_barrier((half, packed, ordered))
    half = lax.all_to_all(half, ("ra", "rb"), split_axis=0, concat_axis=0, tiled=True)
    half = call(
        functools.partial(second_kernel, groups, cols),
        out_shape=shape((groups * peers, 2, lanes), BF16),
        in_specs=[vmem] * 4,
        scratch_shapes=[pltpu.VMEM((2, r2, channels), BF16)] * 2,
    )(half, ordered, weights, packed)
    half = lax.all_to_all(half, ("ra", "rb"), split_axis=0, concat_axis=0, tiled=True)
    piece = call(
        first_back_kernel,
        out_shape=shape((groups, 2 * rows, lanes), BF16),
        in_specs=[vmem, vmem],
    )(first_prop, half)
    piece = lax.all_to_all(piece, "ra", split_axis=0, concat_axis=0, tiled=True)
    out = call(
        functools.partial(last_kernel, groups, cols),
        out_shape=shape((2 * cells, channels), BF16),
        in_specs=[vmem],
        scratch_shapes=[pltpu.VMEM((channels // LANES, 2 * cells, LANES), F32)],
    )(piece)
    return out.reshape(2, rows, cols, channels)


def solution(mesh):
    return jax.shard_map(
        on_device,
        mesh=mesh,
        in_specs=(P(None, "ra", "rb", None), P(), P(), P(None, "ra", "rb"), P(), P()),
        out_specs=P(None, "ra", "rb", None),
        check_vma=False,
    )
```

```python
import functools

import jax
import jax.numpy as jnp
from jax import lax
from jax.experimental import pallas as pl
from jax.experimental.pallas import tpu as pltpu
from jax.sharding import PartitionSpec as P

LANES = 128
BF16 = jnp.bfloat16
F32 = jnp.float32


def dot(left, right):
    return jnp.dot(left, right, preferred_element_type=F32)


def dot_rows(left, right):
    return lax.dot_general(left, right, (((1,), (1,)), ((), ())), preferred_element_type=F32)


def swap_blocks(tiles, width):
    count = len(tiles)
    per_tile = LANES // width
    bits = per_tile.bit_length() - 1
    lane = lax.broadcasted_iota(jnp.int32, tiles[0][0].shape, 1)
    for bit in range(bits):
        step = 1 << bit
        shift = width * step
        keep = (lane & shift) == 0
        fresh = list(tiles)
        for m in range(count):
            if m & step:
                continue
            low, high = tiles[m], tiles[m + step]
            fresh[m] = [jnp.where(keep, a, pltpu.roll(b, shift, 1)) for a, b in zip(low, high)]
            fresh[m + step] = [
                jnp.where(keep, pltpu.roll(a, LANES - shift, 1), b) for a, b in zip(low, high)
            ]
        tiles = fresh
    halves = count // per_tile
    return [
        [tiles[h * per_tile + m % per_tile][m // per_tile] for h in range(halves)]
        for m in range(count)
    ]


def masked_weights(coupling_ref, pattern_ref, term, block):
    channels = coupling_ref.shape[1]
    count = channels // block
    lane = lax.broadcasted_iota(jnp.int32, (block, channels), 1)
    rows = []
    for i in range(count):
        mask = jnp.zeros((block, channels), F32)
        for j in range(count):
            inside = (lane >= j * block) & (lane < (j + 1) * block)
            mask = jnp.where(inside, pattern_ref[term, i, j].astype(F32), mask)
        piece = coupling_ref[term, i * block:(i + 1) * block, :].astype(F32) * mask
        rows.append(piece.astype(BF16))
    return jnp.concatenate(rows, axis=0)


def kick_into(load, weights, factor_of, rows, count, store):
    together = max(1, 512 // rows)
    for first in range(0, count, together):
        blocks = range(first, first + together)
        re, im = load(first * rows, together * rows)
        sum_re = jnp.zeros(re.shape, F32)
        sum_im = jnp.zeros(re.shape, F32)
        for k in range(len(weights)):
            factor = jnp.concatenate([factor_of(k, n) for n in blocks], axis=0)
            sum_re = sum_re + dot_rows(re, weights[k]) * factor
            sum_im = sum_im + dot_rows(im, weights[k]) * factor
        store(first * rows, re.astype(F32) + sum_im, im.astype(F32) - sum_re)


def order(prop_ref, out_ref, inner):
    size = prop_ref.shape[1]
    outer = size // inner
    row = lax.broadcasted_iota(jnp.int32, (size, size), 0)
    col = lax.broadcasted_iota(jnp.int32, (size, size), 1)
    place = (row % outer) * inner + row // outer
    move = jnp.where(col == place, 1.0, 0.0).astype(BF16)
    for part in range(2):
        out_ref[part] = dot(move, dot_rows(prop_ref[part], move).astype(BF16)).astype(BF16)


def halves_of(value):
    return [value[:, h * LANES:(h + 1) * LANES] for h in range(value.shape[1] // LANES)]


def order_kernel(inner, prop_ref, ordered_ref):
    order(prop_ref, ordered_ref, inner)


def first_kick_kernel(groups, amp_ref, coupling_ref, pattern_ref, radial_ref, out_ref, weights_ref,
                      held, moved, kicked):
    terms, rows, cols = radial_ref.shape
    cells = rows * cols
    channels = coupling_ref.shape[1]
    block = channels // pattern_ref.shape[1]
    parts = channels // LANES
    weights = [masked_weights(coupling_ref, pattern_ref, k, block) for k in range(terms)]
    for k in range(terms):
        weights_ref[k] = weights[k]
    for h in range(parts):
        held[h] = amp_ref[:, h * LANES:(h + 1) * LANES].astype(F32)
    for part in range(2):
        for b in range(cols):
            place = pl.ds(part * cells + b, rows, stride=cols)
            moved[part, b * rows:(b + 1) * rows, :] = jnp.concatenate(
                [held[h, place, :] for h in range(parts)], axis=1
            ).astype(BF16)

    def load(start, size):
        return moved[0, start:start + size, :], moved[1, start:start + size, :]

    def store(start, re, im):
        kicked[0, start:start + re.shape[0], :] = re
        kicked[1, start:start + im.shape[0], :] = im

    kick_into(load, weights, lambda k, b: radial_ref[k, :, b:b + 1], rows, cols, store)
    width = channels // groups
    for part in range(2):
        for a in range(0, rows, 16):
            tiles = [
                halves_of(kicked[part, b * rows + a:b * rows + a + 16, :]) for b in range(cols)
            ]
            tiles = swap_blocks(tiles, width)
            for g in range(groups):
                out_ref[g, part * rows + a:part * rows + a + 16, :] = jnp.concatenate(
                    tiles[g], axis=1
                ).astype(BF16)


def complex_dot(p_re, p_im, k_re, k_im):
    return dot(p_re, k_re) - dot(p_im, k_im), dot(p_re, k_im) + dot(p_im, k_re)


def first_forward_kernel(prop_ref, piece_ref, out_ref):
    groups, double, lanes = piece_ref.shape
    rows = double // 2
    k_re = piece_ref[:, :rows, :].reshape(groups * rows, lanes)
    k_im = piece_ref[:, rows:, :].reshape(groups * rows, lanes)
    re, im = complex_dot(prop_ref[0], prop_ref[1], k_re, k_im)
    out_ref[:, 0, :] = re.astype(BF16)
    out_ref[:, 1, :] = im.astype(BF16)


def first_back_kernel(prop_ref, piece_ref, out_ref):
    groups, double, lanes = out_ref.shape
    rows = double // 2
    re, im = complex_dot(prop_ref[0], prop_ref[1], piece_ref[:, 0, :], piece_ref[:, 1, :])
    out_ref[:, :rows, :] = re.astype(BF16).reshape(groups, rows, lanes)
    out_ref[:, rows:, :] = im.astype(BF16).reshape(groups, rows, lanes)


def second_kernel(groups, cols, piece_ref, prop_ref, weights_ref, radial_ref, out_ref, state, kicked):
    terms, channels = weights_ref.shape[0], weights_ref.shape[1]
    width = channels // groups
    peers = piece_ref.shape[0] // groups
    lanes = cols * width
    size = peers * cols
    for part in range(2):
        for s in range(0, peers, 16):
            tiles = []
            for g in range(groups):
                piece = piece_ref[g * peers + s:g * peers + s + 16, part, :]
                piece = piece.astype(F32)
                tiles.append([piece[:, h * LANES:(h + 1) * LANES] for h in range(lanes // LANES)])
            tiles = swap_blocks(tiles, width)
            for b in range(cols):
                state[part, b * peers + s:b * peers + s + 16, :] = jnp.concatenate(
                    tiles[b], axis=1
                ).astype(BF16)
    re, im = complex_dot(prop_ref[0], prop_ref[1], state[0], state[1])
    state[0] = re.astype(BF16)
    state[1] = im.astype(BF16)

    def load(start, size):
        return state[0, start:start + size, :], state[1, start:start + size, :]

    def store(start, new_re, new_im):
        kicked[0, start:start + new_re.shape[0], :] = new_re.astype(BF16)
        kicked[1, start:start + new_im.shape[0], :] = new_im.astype(BF16)

    weights = [weights_ref[k] for k in range(terms)]
    kick_into(
        load, weights, lambda k, b: radial_ref[:, k * cols + b:k * cols + b + 1], peers, cols, store
    )
    re, im = complex_dot(prop_ref[0], prop_ref[1], kicked[0], kicked[1])
    state[0] = re.astype(BF16)
    state[1] = im.astype(BF16)
    for part in range(2):
        for s in range(0, peers, 16):
            tiles = []
            for b in range(cols):
                piece = state[part, b * peers + s:b * peers + s + 16, :].astype(F32)
                tiles.append([piece[:, h * LANES:(h + 1) * LANES] for h in range(channels // LANES)])
            tiles = swap_blocks(tiles, width)
            for g in range(groups):
                out_ref[g * peers + s:g * peers + s + 16, part, :] = (
                    jnp.concatenate(tiles[g], axis=1).astype(BF16)
                )


def last_kernel(groups, cols, piece_ref, out_ref, held):
    channels = out_ref.shape[1]
    cells = out_ref.shape[0] // 2
    rows = cells // cols
    width = channels // groups
    lanes = piece_ref.shape[2]
    for part in range(2):
        for a in range(0, rows, 16):
            tiles = []
            for g in range(groups):
                piece = piece_ref[g, part * rows + a:part * rows + a + 16, :].astype(F32)
                tiles.append([piece[:, h * LANES:(h + 1) * LANES] for h in range(lanes // LANES)])
            tiles = swap_blocks(tiles, width)
            for b in range(cols):
                place = pl.ds(part * cells + a * cols + b, 16, stride=cols)
                for h in range(channels // LANES):
                    held[h, place, :] = tiles[b][h]
    for h in range(channels // LANES):
        out_ref[:, h * LANES:(h + 1) * LANES] = held[h].astype(BF16)


def swap_rows(table, axis, steps):
    size = table.shape[0]
    me = lax.axis_index(axis)
    for step in steps:
        pairs = [(i, i ^ step) for i in range(size)]
        split = table.reshape(size // (2 * step), 2, step, table.shape[1])
        low, high = split[:, 0], split[:, 1]
        upper = (me & step) != 0
        other = lax.ppermute(jnp.where(upper, low, high), axis, pairs)
        low, high = jnp.where(upper, other, low), jnp.where(upper, high, other)
        table = jnp.stack([low, high], axis=1).reshape(table.shape)
    return table


def on_device(amplitude, coupling, pattern, radial, first_prop, second_prop):
    _, rows, cols, channels = amplitude.shape
    cells = rows * cols
    terms = pattern.shape[0]
    groups, peers = lax.axis_size("ra"), lax.axis_size("rb")
    width = channels // groups
    lanes = cols * width
    r1, r2 = first_prop.shape[1], second_prop.shape[1]
    params = pltpu.CompilerParams(vmem_limit_bytes=20 * 1024 * 1024)
    vmem = pl.BlockSpec(memory_space=pltpu.VMEM)
    smem = pl.BlockSpec(memory_space=pltpu.SMEM)
    call = functools.partial(pl.pallas_call, compiler_params=params, out_specs=vmem)
    shape = jax.ShapeDtypeStruct

    packed = radial.transpose(1, 0, 2).reshape(rows, terms * cols)
    packed = jnp.pad(packed, ((0, 0), (0, (-terms * cols) % LANES)))

    packed = swap_rows(packed, "rb", [1])
    piece, weights = pl.pallas_call(
        functools.partial(first_kick_kernel, groups),
        out_shape=[shape((groups, 2 * rows, lanes), BF16), shape(coupling.shape, BF16)],
        in_specs=[vmem, vmem, smem, vmem],
        out_specs=[vmem] * 2,
        scratch_shapes=[
            pltpu.VMEM((channels // LANES, 2 * cells, LANES), F32),
            pltpu.VMEM((2, cells, channels), BF16),
            pltpu.VMEM((2, cells, channels), F32),
        ],
        compiler_params=params,
    )(amplitude.reshape(2 * cells, channels), coupling, pattern, radial)
    packed, weights, second_prop = lax.optimization_barrier((packed, weights, second_prop))
    steps = [1 << bit for bit in range(1, peers.bit_length() - 1)]
    packed = swap_rows(packed, "rb", steps[::-1])
    ordered = call(
        functools.partial(order_kernel, cols),
        out_shape=shape(second_prop.shape, BF16),
        in_specs=[vmem],
    )(second_prop)
    piece = lax.all_to_all(piece, "ra", split_axis=0, concat_axis=0, tiled=True)
    half = call(
        first_forward_kernel,
        out_shape=shape((r1, 2, lanes), BF16),
        in_specs=[vmem, vmem],
    )(first_prop, piece)
    half, packed, ordered = lax.optimization_barrier((half, packed, ordered))
    half = lax.all_to_all(half, ("ra", "rb"), split_axis=0, concat_axis=0, tiled=True)
    half = call(
        functools.partial(second_kernel, groups, cols),
        out_shape=shape((groups * peers, 2, lanes), BF16),
        in_specs=[vmem] * 4,
        scratch_shapes=[pltpu.VMEM((2, r2, channels), BF16)] * 2,
    )(half, ordered, weights, packed)
    half = lax.all_to_all(half, ("ra", "rb"), split_axis=0, concat_axis=0, tiled=True)
    piece = call(
        first_back_kernel,
        out_shape=shape((groups, 2 * rows, lanes), BF16),
        in_specs=[vmem, vmem],
    )(first_prop, half)
    piece = lax.all_to_all(piece, "ra", split_axis=0, concat_axis=0, tiled=True)
    out = call(
        functools.partial(last_kernel, groups, cols),
        out_shape=shape((2 * cells, channels), BF16),
        in_specs=[vmem],
        scratch_shapes=[pltpu.VMEM((channels // LANES, 2 * cells, LANES), F32)],
    )(piece)
    return out.reshape(2, rows, cols, channels)


def solution(mesh):
    return jax.shard_map(
        on_device,
        mesh=mesh,
        in_specs=(P(None, "ra", "rb", None), P(), P(), P(None, "ra", "rb"), P(), P()),
        out_specs=P(None, "ra", "rb", None),
        check_vma=False,
    )
```
